32 devices in a mesh: seq: 8 (over z, y), head: 4 (over x, core).
Axes of the slice: x: 2, y: 2, z: 4, core: 2. Of those that a mesh axis runs over, the one named last changes fastest.
Arguments:
- query: bfloat16 [1024, 64, 576], P('seq', 'head'), may hold values from -10 to 10
- cache: bfloat16 [4096, 576], P('seq'), may hold values from -6 to 6
- grad_out: bfloat16 [1024, 64, 128], P('seq', 'head'), may hold values from -6 to 6
- value_weight: bfloat16 [64, 512, 128], P('head'), may hold values from -0.25 to 0.25
- picked: int32 [32, 4], P('seq'), may hold values from 0 to 31, as said below
Outputs:
- d_query: bfloat16 [1024, 64, 576], P('seq', 'head')
- d_cache: float32 [32, 128, 576], P('seq', 'head')
- d_value_weight: bfloat16 [64, 512, 128], P('head')
The draws below stay inside these ranges and needn't reach their ends.
Inputs may be any that keep to these rules, and one draw needn't show every extreme that they name: `picked`: row g names 4 different blocks, each starting at or before the first query of block g. One of them is the block that holds query block g; every other one ends before position 3072. The rows of one index of seq together name at most 2 different blocks of any one owner (owner o holds blocks o * 4 to o * 4 + 3), and in every draw some owner has exactly 2 of its blocks named by every index of seq.
All inputs are finite; a program needn't handle non-finite values.
Results may differ from the reference program's by a relative error of at most 0.01.
Values may be sent and summed in bfloat16 or wider, within the bound.
A program may use at most 128 MiB of HBM per device.

```python
import jax
import jax.numpy as jnp
from jax import lax

HEADS = 64
KVL = 512
ROPE = 64
VD = 128
BLOCK = 128
QB = 32
TOPB = 4
Q_DEV = 128
QUERIES = 1024
CTX = 4096
QBLOCKS = 32
NBLK_DEV = 4
CAP = 2
FULL = 6


def distinct_order(key, array_shape):
    length = array_shape[-1]
    scores = jax.random.randint(key, array_shape, 0, 1 << 16)
    scores = scores * length + jnp.arange(length, dtype=jnp.int32)
    return jnp.argsort(scores, axis=-1).astype(jnp.int32)


def draw_cache(key, part):
    array_shape = (CTX, KVL + ROPE)
    drawn = jnp.clip(jax.random.normal(jax.random.fold_in(key, 1), array_shape, jnp.float32), -6.0, 6.0)
    return drawn.astype(jnp.bfloat16)


def draw_query(key, part):
    array_shape = (QUERIES, HEADS, KVL + ROPE)
    drawn = jnp.clip(jax.random.normal(jax.random.fold_in(key, 2), array_shape, jnp.float32), -6.0, 6.0)
    return drawn.astype(jnp.bfloat16)


def draw_picked(key, part):
    per_device = Q_DEV // QB
    seq_count = QUERIES // Q_DEV
    candidates_per = FULL * CAP
    local_order = distinct_order(jax.random.fold_in(key, 11), (seq_count, FULL, NBLK_DEV))
    owner_ids = jnp.arange(FULL, dtype=jnp.int32)
    candidates = owner_ids[None, :, None] * NBLK_DEV + local_order[:, :, :CAP]
    hot_owner = jax.random.randint(jax.random.fold_in(key, 12), (), 0, FULL)
    hot_blocks = jnp.take(candidates, hot_owner, axis=1)
    flat_candidates = candidates.reshape(seq_count, candidates_per)
    is_hot = (jnp.arange(candidates_per, dtype=jnp.int32) // CAP == hot_owner).astype(jnp.int32)
    scores = jax.random.randint(jax.random.fold_in(key, 13), (seq_count, per_device, candidates_per), 0, 1 << 16)
    scores = scores * candidates_per + jnp.arange(candidates_per, dtype=jnp.int32) + is_hot * (1 << 28)
    ranking = jnp.argsort(scores, axis=-1)[:, :, :TOPB - 1 - CAP]
    others = jnp.take_along_axis(jnp.broadcast_to(flat_candidates[:, None, :], scores.shape), ranking, axis=-1)
    block_rows = jnp.arange(QBLOCKS, dtype=jnp.int32).reshape(seq_count, per_device)
    own_block = (CTX - QUERIES + block_rows * QB + QB - 1) // BLOCK
    picked_lists = jnp.concatenate([own_block[:, :, None], jnp.broadcast_to(hot_blocks[:, None, :], (seq_count, per_device, CAP)), others], axis=-1)
    placing = distinct_order(jax.random.fold_in(key, 14), (seq_count, per_device, TOPB))
    picked_lists = jnp.take_along_axis(picked_lists, placing, axis=-1)
    return picked_lists.reshape(QBLOCKS, TOPB).astype(jnp.int32)


def levels(key, shape, split, low, high):
    def one(dim, blocks):
        steps = jax.random.uniform(jax.random.fold_in(jax.random.fold_in(key, 6), dim), (blocks,), jnp.float32, low / len(split), high / len(split))
        return jnp.repeat(jnp.exp(steps), shape[dim] // blocks).reshape((-1,) + (1,) * (len(shape) - dim - 1))

    level = one(*split[0])
    for cut in split[1:]:
        level = level * one(*cut)
    return level


def noise(stream_key, shape, deviation, limit, cuts=(), held_as=jnp.bfloat16):
    level = levels(stream_key, shape, cuts, -0.22, 0.18) if cuts else 1.0
    values = jax.random.normal(stream_key, shape, jnp.float32) * deviation * level
    return jnp.minimum(jnp.maximum(values, -limit), limit).astype(held_as)


def setup_inputs(seed: int = 0) -> dict:
    key_of = jax.random.split(jax.random.key(seed), 6)
    return {
        "query": draw_query(jax.random.fold_in(key_of[5], 71), 0),
        "cache": draw_cache(jax.random.fold_in(key_of[5], 71), 0),
        "grad_out": noise(key_of[2], (QUERIES, HEADS, VD), 1.0, 6.0, ((0, 8), (1, 4))),
        "value_weight": noise(key_of[3], (HEADS, KVL, VD), KVL ** -0.5, 0.25, ((0, 4),)),
        "picked": draw_picked(jax.random.fold_in(key_of[5], 71), 0),
    }


SCORE_SCALE = 0.07216878364870323
MASKED = -1.0e30


def block_backward(q_rows, key_rows, d_latent, visible):
    value_rows = key_rows[:, :KVL]
    scores = lax.dot_general(q_rows, key_rows, (((1,), (1,)), ((), ())), preferred_element_type=jnp.float32) * SCORE_SCALE
    scores = jnp.where(visible, scores, MASKED)
    row_max = jnp.max(scores, axis=1, keepdims=True)
    exp_scores = jnp.exp(scores - row_max)
    weights = exp_scores / jnp.sum(exp_scores, axis=1, keepdims=True)
    weights_low = weights.astype(jnp.bfloat16)
    latent_out = jnp.dot(weights_low, value_rows, preferred_element_type=jnp.float32).astype(jnp.bfloat16)
    row_delta = jnp.sum(d_latent.astype(jnp.float32) * latent_out.astype(jnp.float32), axis=1, keepdims=True)
    d_probs = lax.dot_general(d_latent, value_rows, (((1,), (1,)), ((), ())), preferred_element_type=jnp.float32)
    d_scores = (SCORE_SCALE * weights * (d_probs - row_delta)).astype(jnp.bfloat16)
    d_query = jnp.dot(d_scores, key_rows, preferred_element_type=jnp.float32).astype(jnp.bfloat16)
    d_keys = lax.dot_general(d_scores, q_rows, (((0,), (0,)), ((), ())), preferred_element_type=jnp.float32)
    d_values = lax.dot_general(weights_low, d_latent, (((0,), (0,)), ((), ())), preferred_element_type=jnp.float32)
    d_keys = jnp.concatenate([d_keys[:, :KVL] + d_values, d_keys[:, KVL:]], axis=1)
    return d_query, d_keys, latent_out


def reference(query, cache, grad_out, value_weight, picked):
    head_count = query.shape[1]
    row_width = query.shape[2]
    row_count = QB * head_count
    cache_blocks = cache.reshape(CTX // BLOCK, BLOCK, row_width)
    first_pos = CTX - QUERIES
    weight_f = value_weight.astype(jnp.float32)

    def one_block(totals, inputs):
        cache_total, weight_total = totals
        q_block, grad_block, chosen, block_index = inputs
        d_latent = jnp.einsum("qhv,hcv->qhc", grad_block.astype(jnp.float32), weight_f).astype(jnp.bfloat16)
        key_rows = jnp.take(cache_blocks, chosen, axis=0).reshape(TOPB * BLOCK, row_width)
        query_pos = first_pos + block_index * QB + jnp.arange(QB, dtype=jnp.int32)
        row_pos = jnp.repeat(query_pos, head_count)
        key_pos = (chosen[:, None] * BLOCK + jnp.arange(BLOCK, dtype=jnp.int32)[None, :]).reshape(TOPB * BLOCK)
        visible = key_pos[None, :] <= row_pos[:, None]
        d_query, d_keys, latent_out = block_backward(q_block.reshape(row_count, row_width), key_rows, d_latent.reshape(row_count, KVL), visible)
        cache_total = cache_total.at[chosen].add(d_keys.reshape(TOPB, BLOCK, row_width))
        weight_total = weight_total + jnp.einsum("qhc,qhv->hcv", latent_out.reshape(QB, head_count, KVL).astype(jnp.float32), grad_block.astype(jnp.float32))
        return (cache_total, weight_total), d_query.reshape(QB, head_count, row_width)

    start_totals = (jnp.zeros((CTX // BLOCK, BLOCK, row_width), jnp.float32), jnp.zeros((head_count, KVL, VD), jnp.float32))
    inputs = (query.reshape(QBLOCKS, QB, head_count, row_width), grad_out.reshape(QBLOCKS, QB, head_count, VD), picked, jnp.arange(QBLOCKS, dtype=jnp.int32))
    (cache_total, weight_total), d_query = lax.scan(one_block, start_totals, inputs)
    return d_query.reshape(QUERIES, head_count, row_width), cache_total, weight_total.astype(jnp.bfloat16)
```

```python
import functools

import jax
import jax.numpy as jnp
from jax import lax
from jax.experimental import pallas as pl
from jax.experimental.pallas import tpu as pltpu
from jax.sharding import PartitionSpec as P

KVL = 512
BLOCK = 128
QB = 32
TOPB = 4


SCORE_SCALE = 0.07216878364870323
MASKED = -1e30

NT = (((1,), (1,)), ((), ()))


def attention_kernel(
    slot_ref,
    rel_ref,
    q_ref,
    g_ref,
    w_ref,
    kt_ref,
    dq_ref,
    dk_ref,
    wt_ref,
    q_rows,
    dl_rows,
    lo_rows,
    dq_rows,
    kt_all,
    kn_all,
    dk_sum,
):
    heads, width, queries = q_ref.shape
    qblocks = queries // QB
    group = BLOCK // QB
    f32, bf16 = jnp.float32, jnp.bfloat16

    def spread(i, carry):
        lanes = pl.ds(pl.multiple_of(i * BLOCK, BLOCK), BLOCK)
        qs = [q_ref[i * group + j] for j in range(group)]
        ds = [
            lax.dot_general(
                w_ref[i * group + j], g_ref[i * group + j], NT, preferred_element_type=f32
            ).astype(bf16)
            for j in range(group)
        ]
        for g in range(qblocks):
            cut = slice(g * QB, (g + 1) * QB)
            q_rows[g, :, lanes] = jnp.concatenate([x[:, cut] for x in qs], axis=1)
            dl_rows[g, :, lanes] = jnp.concatenate([x[:, cut] for x in ds], axis=1)
        return carry

    lax.fori_loop(0, heads // group, spread, 0)
    dk_sum[...] = jnp.zeros_like(dk_sum)

    def block(g, carry):
        for t in range(TOPB):
            key_t = kt_ref[slot_ref[g * TOPB + t]]
            kt_all[:, t * BLOCK : (t + 1) * BLOCK] = key_t
            kn_all[t * BLOCK : (t + 1) * BLOCK, :] = key_t.T
        q_t = q_rows[g]
        dl_t = dl_rows[g]
        rows = q_t.shape[1]
        scores = jnp.dot(kn_all[...], q_t, preferred_element_type=f32) * SCORE_SCALE
        key_at = lax.broadcasted_iota(jnp.int32, (BLOCK, rows), 0)
        query_at = lax.rem(lax.broadcasted_iota(jnp.int32, (BLOCK, rows), 1), QB)
        ahead = key_at - query_at
        parts = []
        for t in range(TOPB):
            seen = ahead <= -rel_ref[g * TOPB + t]
            parts.append(jnp.where(seen, scores[t * BLOCK : (t + 1) * BLOCK], MASKED))
        scores = jnp.concatenate(parts, axis=0)
        top = jnp.max(scores, axis=0, keepdims=True)
        exps = jnp.exp(scores - top)
        weights = exps / jnp.sum(exps, axis=0, keepdims=True)
        low = weights.astype(bf16)
        latent = jnp.dot(kt_all[:KVL, :], low, preferred_element_type=f32).astype(bf16)
        lo_rows[g] = latent
        delta = jnp.sum(dl_t.astype(f32) * latent.astype(f32), axis=0, keepdims=True)
        d_probs = jnp.dot(kn_all[:, :KVL], dl_t, preferred_element_type=f32)
        d_scores = (SCORE_SCALE * weights * (d_probs - delta)).astype(bf16)
        dq_rows[g] = jnp.dot(kt_all[...], d_scores, preferred_element_type=f32).astype(bf16)
        d_keys = lax.dot_general(d_scores, q_t, NT, preferred_element_type=f32)
        d_values = lax.dot_general(low, dl_t, NT, preferred_element_type=f32)
        for t in range(TOPB):
            slot = slot_ref[g * TOPB + t]
            cut = slice(t * BLOCK, (t + 1) * BLOCK)
            dk_sum[slot, :, :KVL] += d_keys[cut, :KVL] + d_values[cut]
            dk_sum[slot, :, KVL:] += d_keys[cut, KVL:]
        return carry

    lax.fori_loop(0, qblocks, block, 0)
    dk_ref[...] = dk_sum[...].astype(dk_ref.dtype)

    def gather(i, carry):
        lanes = pl.ds(pl.multiple_of(i * BLOCK, BLOCK), BLOCK)
        qs = [dq_rows[g, :, lanes] for g in range(qblocks)]
        ls = [lo_rows[g, :, lanes] for g in range(qblocks)]
        for j in range(group):
            cut = slice(j * QB, (j + 1) * QB)
            dq_ref[i * group + j] = jnp.concatenate([x[:, cut] for x in qs], axis=1)
            latent = jnp.concatenate([x[:, cut] for x in ls], axis=1)
            wt_ref[i * group + j] = jnp.dot(
                latent, g_ref[i * group + j], preferred_element_type=f32
            ).astype(wt_ref.dtype)
        return carry

    lax.fori_loop(0, heads // group, gather, 0)


def attention(slots, rel, q_t, g_h, weight, keys_t):
    heads, width, queries = q_t.shape
    slot_total = keys_t.shape[0]
    qblocks = queries // QB
    rows = heads * QB
    macs = heads * queries * (TOPB * BLOCK * 3 * (width + KVL) + 2 * KVL * BLOCK)
    vmem = pl.BlockSpec(memory_space=pltpu.VMEM)
    smem = pl.BlockSpec(memory_space=pltpu.SMEM)
    bf16 = jnp.bfloat16
    return pl.pallas_call(
        attention_kernel,
        out_shape=(
            jax.ShapeDtypeStruct(q_t.shape, bf16),
            jax.ShapeDtypeStruct((slot_total, BLOCK, width), bf16),
            jax.ShapeDtypeStruct(weight.shape, bf16),
        ),
        in_specs=[smem, smem, vmem, vmem, vmem, vmem],
        out_specs=(vmem, vmem, vmem),
        scratch_shapes=[
            pltpu.VMEM((qblocks, width, rows), bf16),
            pltpu.VMEM((qblocks, KVL, rows), bf16),
            pltpu.VMEM((qblocks, KVL, rows), bf16),
            pltpu.VMEM((qblocks, width, rows), bf16),
            pltpu.VMEM((width, TOPB * BLOCK), bf16),
            pltpu.VMEM((TOPB * BLOCK, width), bf16),
            pltpu.VMEM((slot_total, BLOCK, width), jnp.float32),
        ],
        compiler_params=pltpu.CompilerParams(vmem_limit_bytes=60 << 20),
        cost_estimate=pl.CostEstimate(
            flops=2 * macs, bytes_accessed=16 << 20, transcendentals=rows * qblocks * 512
        ),
        name="attention",
    )(slots, rel, q_t, g_h, weight, keys_t)


def local(query, cache, grad_out, value_weight, picked):
    q_dev, heads_here, row_width = query.shape
    ctx_dev = cache.shape[0]
    owners = lax.axis_size("seq")
    seq_index = lax.axis_index("seq")
    quarters = lax.axis_size("head")
    quarter = lax.axis_index("head")
    block_count = ctx_dev // BLOCK
    qblocks_here = q_dev // QB
    entries = qblocks_here * TOPB
    capacity = max(q_dev // BLOCK, entries // owners)
    slot_total = owners * capacity
    sub_rows = BLOCK // quarters
    sub_cols = row_width // quarters
    flat_pick = picked.reshape(entries)
    owner_of = flat_pick // block_count
    global_ids = jnp.arange(owners * block_count, dtype=jnp.int32)
    matches = flat_pick[:, None] == global_ids[None, :]
    wanted = jnp.any(matches, axis=0).astype(jnp.int32).reshape(owners, block_count)
    order_in = jnp.cumsum(wanted, axis=1) - 1
    slot_ids = jnp.arange(capacity, dtype=jnp.int32)
    local_ids = jnp.arange(block_count, dtype=jnp.int32)
    holding = (wanted[:, None, :] == 1) & (order_in[:, None, :] == slot_ids[None, :, None])
    present = jnp.any(holding, axis=2)
    request = jnp.where(
        present, jnp.sum(jnp.where(holding, local_ids[None, None, :], 0), axis=2), -1
    )
    entry_rank = jnp.sum(
        jnp.where(matches, order_in.reshape(owners * block_count)[None, :], 0), axis=1
    )
    entry_slot = owner_of * capacity + entry_rank
    asked_rows = lax.all_to_all(request, "seq", split_axis=0, concat_axis=0, tiled=True).reshape(
        slot_total
    )
    owner_map = (local_ids[:, None] == asked_rows[None, :]).astype(jnp.float32)
    cache_t = cache.T
    part_t = lax.dynamic_slice_in_dim(cache_t, quarter * sub_cols, sub_cols, 0)
    part_blocks = jnp.stack(
        [part_t[:, b * BLOCK : (b + 1) * BLOCK] for b in range(block_count)]
    )
    packed = jnp.zeros((slot_total, sub_cols, BLOCK), cache.dtype)
    for b in range(block_count):
        packed = jnp.where((asked_rows == b)[:, None, None], part_blocks[b][None], packed)
    fetched = lax.all_to_all(
        packed.reshape(owners, capacity, sub_cols, BLOCK),
        "seq",
        split_axis=0,
        concat_axis=0,
        tiled=True,
    )
    keys_t = lax.all_gather(
        fetched.reshape(slot_total, sub_cols, BLOCK), "head", axis=1, tiled=True
    )
    first_pos = ctx_dev * owners - q_dev * owners + seq_index * q_dev
    rel = flat_pick * BLOCK - first_pos - (jnp.arange(entries, dtype=jnp.int32) // TOPB) * QB
    d_query_t, slot_grads, weight_terms = attention(
        entry_slot,
        rel,
        jnp.transpose(query, (1, 2, 0)),
        jnp.transpose(grad_out, (1, 0, 2)),
        value_weight,
        keys_t,
    )
    flat = weight_terms.reshape(owners, -1, weight_terms.shape[2])
    swapped = lax.all_to_all(flat, "seq", split_axis=0, concat_axis=0, tiled=True)
    summed = jnp.sum(swapped.astype(jnp.float32), axis=0).astype(jnp.bfloat16)
    d_value_weight = lax.all_gather(summed, "seq", axis=0, tiled=True).reshape(value_weight.shape)
    shares = lax.psum_scatter(slot_grads, "head", scatter_dimension=1, tiled=True)
    returned = lax.all_to_all(
        shares.reshape(owners, capacity, sub_rows, row_width),
        "seq",
        split_axis=0,
        concat_axis=0,
        tiled=True,
    )
    d_cache = jnp.dot(
        owner_map,
        returned.astype(jnp.float32).reshape(slot_total, sub_rows * row_width),
        precision=lax.Precision.HIGHEST,
    ).reshape(block_count, sub_rows, row_width)
    return (jnp.transpose(d_query_t, (2, 0, 1)), d_cache, d_value_weight)


def solution(mesh):
    in_specs = (
        P("seq", "head", None),
        P("seq", None),
        P("seq", "head", None),
        P("head", None, None),
        P("seq", None),
    )
    out_specs = (P("seq", "head", None), P("seq", "head", None), P("head", None, None))
    return jax.shard_map(local, mesh=mesh, in_specs=in_specs, out_specs=out_specs, check_vma=False)
```

```python
import functools

import jax
import jax.numpy as jnp
from jax import lax
from jax.experimental import pallas as pl
from jax.experimental.pallas import tpu as pltpu
from jax.sharding import PartitionSpec as P

KVL = 512
BLOCK = 128
QB = 32
TOPB = 4


SCORE_SCALE = 0.07216878364870323
MASKED = -1e30

NT = (((1,), (1,)), ((), ()))


def attention_kernel(
    slot_ref,
    rel_ref,
    q_ref,
    g_ref,
    w_ref,
    kt_ref,
    dq_ref,
    dk_ref,
    wt_ref,
    q_rows,
    dl_rows,
    lo_rows,
    dq_rows,
    kt_all,
    kn_all,
    dk_sum,
):
    heads, width, queries = q_ref.shape
    qblocks = queries // QB
    group = BLOCK // QB
    f32, bf16 = jnp.float32, jnp.bfloat16

    def spread(i, carry):
        lanes = pl.ds(pl.multiple_of(i * BLOCK, BLOCK), BLOCK)
        qs = [q_ref[i * group + j] for j in range(group)]
        ds = [
            lax.dot_general(
                w_ref[i * group + j], g_ref[i * group + j], NT, preferred_element_type=f32
            ).astype(bf16)
            for j in range(group)
        ]
        for g in range(qblocks):
            cut = slice(g * QB, (g + 1) * QB)
            q_rows[g, :, lanes] = jnp.concatenate([x[:, cut] for x in qs], axis=1)
            dl_rows[g, :, lanes] = jnp.concatenate([x[:, cut] for x in ds], axis=1)
        return carry

    lax.fori_loop(0, heads // group, spread, 0)
    dk_sum[...] = jnp.zeros_like(dk_sum)

    def block(g, carry):
        for t in range(TOPB):
            key_t = kt_ref[slot_ref[g * TOPB + t]]
            kt_all[:, t * BLOCK : (t + 1) * BLOCK] = key_t
            kn_all[t * BLOCK : (t + 1) * BLOCK, :] = key_t.T
        q_t = q_rows[g]
        dl_t = dl_rows[g]
        rows = q_t.shape[1]
        scores = jnp.dot(kn_all[...], q_t, preferred_element_type=f32) * SCORE_SCALE
        key_at = lax.broadcasted_iota(jnp.int32, (BLOCK, rows), 0)
        query_at = lax.rem(lax.broadcasted_iota(jnp.int32, (BLOCK, rows), 1), QB)
        ahead = key_at - query_at
        parts = []
        for t in range(TOPB):
            seen = ahead <= -rel_ref[g * TOPB + t]
            parts.append(jnp.where(seen, scores[t * BLOCK : (t + 1) * BLOCK], MASKED))
        scores = jnp.concatenate(parts, axis=0)
        top = jnp.max(scores, axis=0, keepdims=True)
        exps = jnp.exp(scores - top)
        weights = exps / jnp.sum(exps, axis=0, keepdims=True)
        low = weights.astype(bf16)
        latent = jnp.dot(kt_all[:KVL, :], low, preferred_element_type=f32).astype(bf16)
        lo_rows[g] = latent
        delta = jnp.sum(dl_t.astype(f32) * latent.astype(f32), axis=0, keepdims=True)
        d_probs = jnp.dot(kn_all[:, :KVL], dl_t, preferred_element_type=f32)
        d_scores = (SCORE_SCALE * weights * (d_probs - delta)).astype(bf16)
        dq_rows[g] = jnp.dot(kt_all[...], d_scores, preferred_element_type=f32).astype(bf16)
        d_keys = lax.dot_general(d_scores, q_t, NT, preferred_element_type=f32)
        d_values = lax.dot_general(low, dl_t, NT, preferred_element_type=f32)
        for t in range(TOPB):
            slot = slot_ref[g * TOPB + t]
            cut = slice(t * BLOCK, (t + 1) * BLOCK)
            dk_sum[slot, :, :KVL] += d_keys[cut, :KVL] + d_values[cut]
            dk_sum[slot, :, KVL:] += d_keys[cut, KVL:]
        return carry

    lax.fori_loop(0, qblocks, block, 0)
    dk_ref[...] = dk_sum[...].astype(dk_ref.dtype)

    def gather(i, carry):
        lanes = pl.ds(pl.multiple_of(i * BLOCK, BLOCK), BLOCK)
        qs = [dq_rows[g, :, lanes] for g in range(qblocks)]
        ls = [lo_rows[g, :, lanes] for g in range(qblocks)]
        for j in range(group):
            cut = slice(j * QB, (j + 1) * QB)
            dq_ref[i * group + j] = jnp.concatenate([x[:, cut] for x in qs], axis=1)
            latent = jnp.concatenate([x[:, cut] for x in ls], axis=1)
            wt_ref[i * group + j] = jnp.dot(
                latent, g_ref[i * group + j], preferred_element_type=f32
            ).astype(wt_ref.dtype)
        return carry

    lax.fori_loop(0, heads // group, gather, 0)


def attention(slots, rel, q_t, g_h, weight, keys_t):
    heads, width, queries = q_t.shape
    slot_total = keys_t.shape[0]
    qblocks = queries // QB
    rows = heads * QB
    macs = heads * queries * (TOPB * BLOCK * 3 * (width + KVL) + 2 * KVL * BLOCK)
    vmem = pl.BlockSpec(memory_space=pltpu.VMEM)
    smem = pl.BlockSpec(memory_space=pltpu.SMEM)
    bf16 = jnp.bfloat16
    return pl.pallas_call(
        attention_kernel,
        out_shape=(
            jax.ShapeDtypeStruct(q_t.shape, bf16),
            jax.ShapeDtypeStruct((slot_total, BLOCK, width), bf16),
            jax.ShapeDtypeStruct(weight.shape, bf16),
        ),
        in_specs=[smem, smem, vmem, vmem, vmem, vmem],
        out_specs=(vmem, vmem, vmem),
        scratch_shapes=[
            pltpu.VMEM((qblocks, width, rows), bf16),
            pltpu.VMEM((qblocks, KVL, rows), bf16),
            pltpu.VMEM((qblocks, KVL, rows), bf16),
            pltpu.VMEM((qblocks, width, rows), bf16),
            pltpu.VMEM((width, TOPB * BLOCK), bf16),
            pltpu.VMEM((TOPB * BLOCK, width), bf16),
            pltpu.VMEM((slot_total, BLOCK, width), jnp.float32),
        ],
        compiler_params=pltpu.CompilerParams(vmem_limit_bytes=60 << 20),
        cost_estimate=pl.CostEstimate(
            flops=2 * macs, bytes_accessed=16 << 20, transcendentals=rows * qblocks * 512
        ),
        name="attention",
    )(slots, rel, q_t, g_h, weight, keys_t)


PIECES = 4


def reduce_kernel(
    owners,
    quarters,
    w_ref,
    dk_ref,
    out_ref,
    ret_ref,
    y_buf,
    z_send,
    z_buf,
    mine,
    kept,
    half_buf,
    final,
    y_sem,
    z_sem,
    gz_sem,
    gy_sem,
    half_sem,
    ret_sem,
):
    f32, bf16 = jnp.float32, jnp.bfloat16
    s = lax.axis_index("seq")
    h = lax.axis_index("head")
    outer = owners // 2
    a, b = s // 2, lax.rem(s, 2)
    pair = a * 2 + 1 - b
    cap = ret_ref.shape[1]
    sub = ret_ref.shape[2]
    rows = w_ref.shape[1] // PIECES
    bits = []
    while (1 << len(bits)) < quarters:
        bits.append(1 << len(bits))

    def flipped(bit):
        return h + bit * (1 - 2 * lax.rem(h // bit, 2))

    barrier = pltpu.get_barrier_semaphore()
    for k in range(owners - 1):
        pl.semaphore_signal(
            barrier,
            inc=1,
            device_id=(lax.rem(s + k + 1, owners), h),
            device_id_type=pl.DeviceIdType.MESH,
        )
    for bit in bits:
        pl.semaphore_signal(
            barrier, inc=1, device_id=(s, flipped(bit)), device_id_type=pl.DeviceIdType.MESH
        )
    pl.semaphore_wait(barrier, owners - 1 + len(bits))

    def send(src, dst, sems, index, target):
        copy = pltpu.make_async_remote_copy(
            src_ref=src,
            dst_ref=dst,
            send_sem=sems.at[(0,) + index],
            recv_sem=sems.at[(1,) + index],
            device_id=target,
            device_id_type=pl.DeviceIdType.MESH,
        )
        copy.start()
        return copy

    def ahead(k):
        return lax.rem(a + k + 1, outer)

    def behind(k):
        return lax.rem(a + outer - k - 1, outer)

    def owner(k):
        return lax.rem(s + k + 1, owners)

    cuts = [pl.ds(p * rows, rows) for p in range(PIECES)]
    y_copy, z_copy, gz_copy, gy_copy = {}, {}, {}, {}
    half_copy, ret_copy = {}, {}

    first = bits[0]
    low = lax.rem(h, 2)
    for k in range(outer):
        y_copy[0, k] = send(
            w_ref.at[ahead(k) * 2 + 1 - b, cuts[0]], y_buf.at[0, k], y_sem, (0, k), (pair, h)
        )
    for k in range(owners):
        slots = pl.ds(owner(k) * cap, cap)
        for i in range(quarters // 2):
            q = 2 * i + 1 - low
            half_copy[0, k, i] = send(
                dk_ref.at[slots, pl.ds(pl.multiple_of(q * sub, sub), sub)],
                half_buf.at[0, k, i],
                half_sem,
                (0, k, i),
                (s, flipped(first)),
            )
    for p in range(1, PIECES):
        for k in range(outer):
            y_copy[p, k] = send(
                w_ref.at[ahead(k) * 2 + 1 - b, cuts[p]], y_buf.at[p, k], y_sem, (p, k), (pair, h)
            )

    def halve(level, k):
        bit = bits[level]
        count = quarters // (2 * bit)
        for i in range(count):
            half_copy[level, k, i].wait_recv()
            if level == 0:
                q = 2 * i + low
                here = dk_ref[
                    pl.ds(owner(k) * cap, cap), pl.ds(pl.multiple_of(q * sub, sub), sub)
                ].astype(f32)
            else:
                here = kept[level - 1, k, 2 * i + lax.rem(h // bit, 2)].astype(f32)
            here = here + half_buf[level, k, i].astype(f32)
            if level + 1 < len(bits):
                kept[level, k, i] = here.astype(bf16)
        if level + 1 < len(bits):
            after = bits[level + 1]
            for i in range(count // 2):
                other = 2 * i + 1 - lax.rem(h // after, 2)
                half_copy[level + 1, k, i] = send(
                    kept.at[level, k, other],
                    half_buf.at[level + 1, k, i],
                    half_sem,
                    (level + 1, k, i),
                    (s, flipped(after)),
                )
        elif k < owners - 1:
            final[k] = here.astype(bf16)
            ret_copy[k] = send(final.at[k], ret_ref.at[s], ret_sem, (k,), (owner(k), h))
        else:
            ret_ref[s] = here.astype(bf16)

    def paired(p):
        for k in range(outer):
            y_copy[p, k].wait_recv()
            part = w_ref[ahead(k) * 2 + b, cuts[p]].astype(f32) + y_buf[p, k].astype(f32)
            if k < outer - 1:
                z_send[p, k] = part.astype(bf16)
                z_copy[p, k] = send(
                    z_send.at[p, k], z_buf.at[p, k], z_sem, (p, k), (ahead(k) * 2 + b, h)
                )
            else:
                mine[p] = part

    def totalled(p):
        total = mine[p]
        for k in range(outer - 1):
            z_copy[p, k].wait_recv()
            total = total + z_buf[p, k].astype(f32)
        out_ref[s, cuts[p]] = total.astype(bf16)
        spot = out_ref.at[s, cuts[p]]
        for k in range(outer - 1):
            gz_copy[p, k] = send(spot, spot, gz_sem, (p, k), (ahead(k) * 2 + b, h))
        gy_copy[p, outer - 1] = send(spot, spot, gy_sem, (p, outer - 1), (pair, h))

    def forwarded(p):
        for k in range(outer - 1):
            gz_copy[p, k].wait_recv()
            spot = out_ref.at[behind(k) * 2 + b, cuts[p]]
            gy_copy[p, k] = send(spot, spot, gy_sem, (p, k), (pair, h))

    for level in range(len(bits) - 1):
        for k in range(owners):
            halve(level, k)
    share = -(-owners // PIECES)
    for p in range(PIECES):
        paired(p)
        for k in range(p * share, min(owners, (p + 1) * share)):
            halve(len(bits) - 1, k)
        if p >= 1:
            totalled(p - 1)
        if p >= 2:
            forwarded(p - 2)
    totalled(PIECES - 1)
    for p in range(max(0, PIECES - 2), PIECES):
        forwarded(p)
    for copy in gy_copy.values():
        copy.wait_recv()
    for copy in ret_copy.values():
        copy.wait_recv()
    for group in (y_copy, z_copy, gz_copy, gy_copy, half_copy, ret_copy):
        for copy in group.values():
            copy.wait_send()


def reduce_all(owners, quarters, weight_terms, slot_grads):
    _, rows, lanes = weight_terms.shape
    slot_total, block, width = slot_grads.shape
    cap = slot_total // owners
    sub = block // quarters
    outer = owners // 2
    levels = max(1, quarters.bit_length() - 1)
    piece = rows // PIECES
    vmem = pl.BlockSpec(memory_space=pltpu.VMEM)
    bf16, f32 = jnp.bfloat16, jnp.float32
    dma = pltpu.SemaphoreType.DMA
    half = quarters // 2
    return pl.pallas_call(
        functools.partial(reduce_kernel, owners, quarters),
        out_shape=(
            jax.ShapeDtypeStruct(weight_terms.shape, bf16),
            jax.ShapeDtypeStruct((owners, cap, sub, width), bf16),
        ),
        in_specs=[vmem, vmem],
        out_specs=(vmem, vmem),
        scratch_shapes=[
            pltpu.VMEM((PIECES, outer, piece, lanes), bf16),
            pltpu.VMEM((PIECES, outer, piece, lanes), bf16),
            pltpu.VMEM((PIECES, outer, piece, lanes), bf16),
            pltpu.VMEM((PIECES, piece, lanes), f32),
            pltpu.VMEM((levels, owners, half, cap, sub, width), bf16),
            pltpu.VMEM((levels, owners, half, cap, sub, width), bf16),
            pltpu.VMEM((owners, cap, sub, width), bf16),
            dma((2, PIECES, outer)),
            dma((2, PIECES, outer)),
            dma((2, PIECES, outer)),
            dma((2, PIECES, outer)),
            dma((2, levels, owners, half)),
            dma((2, owners)),
        ],
        compiler_params=pltpu.CompilerParams(
            collective_id=0, has_side_effects=True, vmem_limit_bytes=60 << 20
        ),
        cost_estimate=pl.CostEstimate(flops=1 << 24, bytes_accessed=16 << 20, transcendentals=0),
        name="reduce_all",
    )(weight_terms, slot_grads)


def local(query, cache, grad_out, value_weight, picked):
    q_dev, heads_here, row_width = query.shape
    ctx_dev = cache.shape[0]
    owners = lax.axis_size("seq")
    seq_index = lax.axis_index("seq")
    quarters = lax.axis_size("head")
    quarter = lax.axis_index("head")
    block_count = ctx_dev // BLOCK
    qblocks_here = q_dev // QB
    entries = qblocks_here * TOPB
    capacity = max(q_dev // BLOCK, entries // owners)
    slot_total = owners * capacity
    sub_rows = BLOCK // quarters
    sub_cols = row_width // quarters
    flat_pick = picked.reshape(entries)
    owner_of = flat_pick // block_count
    global_ids = jnp.arange(owners * block_count, dtype=jnp.int32)
    matches = flat_pick[:, None] == global_ids[None, :]
    wanted = jnp.any(matches, axis=0).astype(jnp.int32).reshape(owners, block_count)
    order_in = jnp.cumsum(wanted, axis=1) - 1
    slot_ids = jnp.arange(capacity, dtype=jnp.int32)
    local_ids = jnp.arange(block_count, dtype=jnp.int32)
    holding = (wanted[:, None, :] == 1) & (order_in[:, None, :] == slot_ids[None, :, None])
    present = jnp.any(holding, axis=2)
    request = jnp.where(
        present, jnp.sum(jnp.where(holding, local_ids[None, None, :], 0), axis=2), -1
    )
    entry_rank = jnp.sum(
        jnp.where(matches, order_in.reshape(owners * block_count)[None, :], 0), axis=1
    )
    entry_slot = owner_of * capacity + entry_rank
    asked_rows = lax.all_to_all(request, "seq", split_axis=0, concat_axis=0, tiled=True).reshape(
        slot_total
    )
    owner_map = (local_ids[:, None] == asked_rows[None, :]).astype(jnp.float32)
    cache_t = cache.T
    part_t = lax.dynamic_slice_in_dim(cache_t, quarter * sub_cols, sub_cols, 0)
    part_blocks = jnp.stack(
        [part_t[:, b * BLOCK : (b + 1) * BLOCK] for b in range(block_count)]
    )
    packed = jnp.zeros((slot_total, sub_cols, BLOCK), cache.dtype)
    for b in range(block_count):
        packed = jnp.where((asked_rows == b)[:, None, None], part_blocks[b][None], packed)
    fetched = lax.all_to_all(
        packed.reshape(owners, capacity, sub_cols, BLOCK),
        "seq",
        split_axis=0,
        concat_axis=0,
        tiled=True,
    )
    keys_t = lax.all_gather(
        fetched.reshape(slot_total, sub_cols, BLOCK), "head", axis=1, tiled=True
    )
    first_pos = ctx_dev * owners - q_dev * owners + seq_index * q_dev
    rel = flat_pick * BLOCK - first_pos - (jnp.arange(entries, dtype=jnp.int32) // TOPB) * QB
    d_query_t, slot_grads, weight_terms = attention(
        entry_slot,
        rel,
        jnp.transpose(query, (1, 2, 0)),
        jnp.transpose(grad_out, (1, 0, 2)),
        value_weight,
        keys_t,
    )
    d_value_weight, returned = reduce_all(
        owners,
        quarters,
        weight_terms.reshape(owners, -1, weight_terms.shape[2]),
        slot_grads,
    )
    d_value_weight = d_value_weight.reshape(value_weight.shape)
    d_cache = jnp.dot(
        owner_map,
        returned.astype(jnp.float32).reshape(slot_total, sub_rows * row_width),
        precision=lax.Precision.HIGHEST,
    ).reshape(block_count, sub_rows, row_width)
    return (jnp.transpose(d_query_t, (2, 0, 1)), d_cache, d_value_weight)


def solution(mesh):
    in_specs = (
        P("seq", "head", None),
        P("seq", None),
        P("seq", "head", None),
        P("head", None, None),
        P("seq", None),
    )
    out_specs = (P("seq", "head", None), P("seq", "head", None), P("head", None, None))
    return jax.shard_map(local, mesh=mesh, in_specs=in_specs, out_specs=out_specs, check_vma=False)
```

```python
import functools

import jax
import jax.numpy as jnp
from jax import lax
from jax.experimental import pallas as pl
from jax.experimental.pallas import tpu as pltpu
from jax.sharding import PartitionSpec as P

KVL = 512
BLOCK = 128
QB = 32
TOPB = 4


SCORE_SCALE = 0.07216878364870323
MASKED = -1e30

NT = (((1,), (1,)), ((), ()))


def attention_kernel(
    slot_ref,
    rel_ref,
    q_ref,
    g_ref,
    w_ref,
    kt_ref,
    dq_ref,
    dk_ref,
    wt_ref,
    q_rows,
    dl_rows,
    lo_rows,
    dq_rows,
    kt_all,
    kn_all,
    dk_sum,
):
    heads, width, queries = q_ref.shape
    qblocks = queries // QB
    group = BLOCK // QB
    f32, bf16 = jnp.float32, jnp.bfloat16

    def spread(i, carry):
        lanes = pl.ds(pl.multiple_of(i * BLOCK, BLOCK), BLOCK)
        qs = [q_ref[i * group + j] for j in range(group)]
        ds = [
            lax.dot_general(
                w_ref[i * group + j], g_ref[i * group + j], NT, preferred_element_type=f32
            ).astype(bf16)
            for j in range(group)
        ]
        for g in range(qblocks):
            cut = slice(g * QB, (g + 1) * QB)
            q_rows[g, :, lanes] = jnp.concatenate([x[:, cut] for x in qs], axis=1)
            dl_rows[g, :, lanes] = jnp.concatenate([x[:, cut] for x in ds], axis=1)
        return carry

    lax.fori_loop(0, heads // group, spread, 0)
    dk_sum[...] = jnp.zeros_like(dk_sum)

    def block(g, carry):
        for t in range(TOPB):
            key_t = kt_ref[slot_ref[g * TOPB + t]]
            kt_all[:, t * BLOCK : (t + 1) * BLOCK] = key_t
            kn_all[t * BLOCK : (t + 1) * BLOCK, :] = key_t.T
        q_t = q_rows[g]
        dl_t = dl_rows[g]
        rows = q_t.shape[1]
        scores = jnp.dot(kn_all[...], q_t, preferred_element_type=f32) * SCORE_SCALE
        key_at = lax.broadcasted_iota(jnp.int32, (BLOCK, rows), 0)
        query_at = lax.rem(lax.broadcasted_iota(jnp.int32, (BLOCK, rows), 1), QB)
        ahead = key_at - query_at
        parts = []
        for t in range(TOPB):
            seen = ahead <= -rel_ref[g * TOPB + t]
            parts.append(jnp.where(seen, scores[t * BLOCK : (t + 1) * BLOCK], MASKED))
        scores = jnp.concatenate(parts, axis=0)
        top = jnp.max(scores, axis=0, keepdims=True)
        exps = jnp.exp(scores - top)
        weights = exps / jnp.sum(exps, axis=0, keepdims=True)
        low = weights.astype(bf16)
        latent = jnp.dot(kt_all[:KVL, :], low, preferred_element_type=f32).astype(bf16)
        lo_rows[g] = latent
        delta = jnp.sum(dl_t.astype(f32) * latent.astype(f32), axis=0, keepdims=True)
        d_probs = jnp.dot(kn_all[:, :KVL], dl_t, preferred_element_type=f32)
        d_scores = (SCORE_SCALE * weights * (d_probs - delta)).astype(bf16)
        dq_rows[g] = jnp.dot(kt_all[...], d_scores, preferred_element_type=f32).astype(bf16)
        d_keys = lax.dot_general(d_scores, q_t, NT, preferred_element_type=f32)
        d_values = lax.dot_general(low, dl_t, NT, preferred_element_type=f32)
        for t in range(TOPB):
            slot = slot_ref[g * TOPB + t]
            cut = slice(t * BLOCK, (t + 1) * BLOCK)
            dk_sum[slot, :, :KVL] += d_keys[cut, :KVL] + d_values[cut]
            dk_sum[slot, :, KVL:] += d_keys[cut, KVL:]
        return carry

    lax.fori_loop(0, qblocks, block, 0)
    dk_ref[...] = dk_sum[...].astype(dk_ref.dtype)

    def gather(i, carry):
        lanes = pl.ds(pl.multiple_of(i * BLOCK, BLOCK), BLOCK)
        qs = [dq_rows[g, :, lanes] for g in range(qblocks)]
        ls = [lo_rows[g, :, lanes] for g in range(qblocks)]
        for j in range(group):
            cut = slice(j * QB, (j + 1) * QB)
            dq_ref[i * group + j] = jnp.concatenate([x[:, cut] for x in qs], axis=1)
            latent = jnp.concatenate([x[:, cut] for x in ls], axis=1)
            wt_ref[i * group + j] = jnp.dot(
                latent, g_ref[i * group + j], preferred_element_type=f32
            ).astype(wt_ref.dtype)
        return carry

    lax.fori_loop(0, heads // group, gather, 0)


def attention(slots, rel, q_t, g_h, weight, keys_t):
    heads, width, queries = q_t.shape
    slot_total = keys_t.shape[0]
    qblocks = queries // QB
    rows = heads * QB
    macs = heads * queries * (TOPB * BLOCK * 3 * (width + KVL) + 2 * KVL * BLOCK)
    vmem = pl.BlockSpec(memory_space=pltpu.VMEM)
    smem = pl.BlockSpec(memory_space=pltpu.SMEM)
    bf16 = jnp.bfloat16
    return pl.pallas_call(
        attention_kernel,
        out_shape=(
            jax.ShapeDtypeStruct(q_t.shape, bf16),
            jax.ShapeDtypeStruct((slot_total, BLOCK, width), bf16),
            jax.ShapeDtypeStruct(weight.shape, bf16),
        ),
        in_specs=[smem, smem, vmem, vmem, vmem, vmem],
        out_specs=(vmem, vmem, vmem),
        scratch_shapes=[
            pltpu.VMEM((qblocks, width, rows), bf16),
            pltpu.VMEM((qblocks, KVL, rows), bf16),
            pltpu.VMEM((qblocks, KVL, rows), bf16),
            pltpu.VMEM((qblocks, width, rows), bf16),
            pltpu.VMEM((width, TOPB * BLOCK), bf16),
            pltpu.VMEM((TOPB * BLOCK, width), bf16),
            pltpu.VMEM((slot_total, BLOCK, width), jnp.float32),
        ],
        compiler_params=pltpu.CompilerParams(vmem_limit_bytes=60 << 20),
        cost_estimate=pl.CostEstimate(
            flops=2 * macs, bytes_accessed=16 << 20, transcendentals=rows * qblocks * 512
        ),
        name="attention",
    )(slots, rel, q_t, g_h, weight, keys_t)


PIECES = 4


def reduce_kernel(
    owners,
    quarters,
    w_ref,
    dk_ref,
    out_ref,
    ret_ref,
    y_buf,
    z_send,
    z_buf,
    mine,
    kept,
    half_buf,
    final,
    y_sem,
    z_sem,
    gz_sem,
    gy_sem,
    half_sem,
    ret_sem,
):
    f32, bf16 = jnp.float32, jnp.bfloat16
    s = lax.axis_index("seq")
    h = lax.axis_index("head")
    outer = owners // 2
    a, b = s // 2, lax.rem(s, 2)
    pair = a * 2 + 1 - b
    cap = ret_ref.shape[1]
    sub = ret_ref.shape[2]
    rows = w_ref.shape[1] // PIECES
    bits = []
    while (1 << len(bits)) < quarters:
        bits.append(1 << len(bits))

    def flipped(bit):
        return h + bit * (1 - 2 * lax.rem(h // bit, 2))

    barrier = pltpu.get_barrier_semaphore()
    for k in range(owners - 1):
        pl.semaphore_signal(
            barrier,
            inc=1,
            device_id=(lax.rem(s + k + 1, owners), h),
            device_id_type=pl.DeviceIdType.MESH,
        )
    for bit in bits:
        pl.semaphore_signal(
            barrier, inc=1, device_id=(s, flipped(bit)), device_id_type=pl.DeviceIdType.MESH
        )
    pl.semaphore_wait(barrier, owners - 1 + len(bits))

    def send(src, dst, sems, index, target):
        copy = pltpu.make_async_remote_copy(
            src_ref=src,
            dst_ref=dst,
            send_sem=sems.at[(0,) + index],
            recv_sem=sems.at[(1,) + index],
            device_id=target,
            device_id_type=pl.DeviceIdType.MESH,
        )
        copy.start()
        return copy

    def ahead(k):
        return lax.rem(a + k + 1, outer)

    def behind(k):
        return lax.rem(a + outer - k - 1, outer)

    def owner(k):
        return lax.rem(s + k + 1, owners)

    cuts = [pl.ds(p * rows, rows) for p in range(PIECES)]
    y_copy, z_copy, gz_copy, gy_copy = {}, {}, {}, {}
    half_copy, ret_copy = {}, {}

    first = bits[0]
    low = lax.rem(h, 2)
    for k in range(outer):
        y_copy[0, k] = send(
            w_ref.at[ahead(k) * 2 + 1 - b, cuts[0]], y_buf.at[0, k], y_sem, (0, k), (pair, h)
        )
    for k in range(owners):
        slots = pl.ds(owner(k) * cap, cap)
        for i in range(quarters // 2):
            q = 2 * i + 1 - low
            half_copy[0, k, i] = send(
                dk_ref.at[slots, pl.ds(pl.multiple_of(q * sub, sub), sub)],
                half_buf.at[0, k, i],
                half_sem,
                (0, k, i),
                (s, flipped(first)),
            )
    for p in range(1, PIECES):
        for k in range(outer):
            y_copy[p, k] = send(
                w_ref.at[ahead(k) * 2 + 1 - b, cuts[p]], y_buf.at[p, k], y_sem, (p, k), (pair, h)
            )

    def halve(level, k):
        bit = bits[level]
        count = quarters // (2 * bit)
        for i in range(count):
            half_copy[level, k, i].wait_recv()
            if level == 0:
                q = 2 * i + low
                here = dk_ref[
                    pl.ds(owner(k) * cap, cap), pl.ds(pl.multiple_of(q * sub, sub), sub)
                ].astype(f32)
            else:
                here = kept[level - 1, k, 2 * i + lax.rem(h // bit, 2)].astype(f32)
            here = here + half_buf[level, k, i].astype(f32)
            if level + 1 < len(bits):
                kept[level, k, i] = here.astype(bf16)
        if level + 1 < len(bits):
            after = bits[level + 1]
            for i in range(count // 2):
                other = 2 * i + 1 - lax.rem(h // after, 2)
                half_copy[level + 1, k, i] = send(
                    kept.at[level, k, other],
                    half_buf.at[level + 1, k, i],
                    half_sem,
                    (level + 1, k, i),
                    (s, flipped(after)),
                )
        elif k < owners - 1:
            final[k] = here.astype(bf16)
            ret_copy[k] = send(final.at[k], ret_ref.at[s], ret_sem, (k,), (owner(k), h))
        else:
            ret_ref[s] = here.astype(bf16)

    def paired(p):
        for k in range(outer):
            y_copy[p, k].wait_recv()
            part = w_ref[ahead(k) * 2 + b, cuts[p]].astype(f32) + y_buf[p, k].astype(f32)
            if k < outer - 1:
                z_send[p, k] = part.astype(bf16)
                z_copy[p, k] = send(
                    z_send.at[p, k], z_buf.at[p, k], z_sem, (p, k), (ahead(k) * 2 + b, h)
                )
            else:
                mine[p] = part

    def totalled(p):
        total = mine[p]
        for k in range(outer - 1):
            z_copy[p, k].wait_recv()
            total = total + z_buf[p, k].astype(f32)
        out_ref[s, cuts[p]] = total.astype(bf16)
        spot = out_ref.at[s, cuts[p]]
        for k in range(outer - 1):
            gz_copy[p, k] = send(spot, spot, gz_sem, (p, k), (ahead(k) * 2 + b, h))
        gy_copy[p, outer - 1] = send(spot, spot, gy_sem, (p, outer - 1), (pair, h))

    def forwarded(p):
        for k in range(outer - 1):
            gz_copy[p, k].wait_recv()
            spot = out_ref.at[behind(k) * 2 + b, cuts[p]]
            gy_copy[p, k] = send(spot, spot, gy_sem, (p, k), (pair, h))

    for level in range(len(bits) - 1):
        for k in range(owners):
            halve(level, k)
    share = -(-owners // PIECES)
    for p in range(PIECES):
        paired(p)
        for k in range(p * share, min(owners, (p + 1) * share)):
            halve(len(bits) - 1, k)
        if p >= 1:
            totalled(p - 1)
        if p >= 2:
            forwarded(p - 2)
    totalled(PIECES - 1)
    for p in range(max(0, PIECES - 2), PIECES):
        forwarded(p)
    for copy in gy_copy.values():
        copy.wait_recv()
    for copy in ret_copy.values():
        copy.wait_recv()
    for group in (y_copy, z_copy, gz_copy, gy_copy, half_copy, ret_copy):
        for copy in group.values():
            copy.wait_send()


def reduce_all(owners, quarters, weight_terms, slot_grads):
    _, rows, lanes = weight_terms.shape
    slot_total, block, width = slot_grads.shape
    cap = slot_total // owners
    sub = block // quarters
    outer = owners // 2
    levels = max(1, quarters.bit_length() - 1)
    piece = rows // PIECES
    vmem = pl.BlockSpec(memory_space=pltpu.VMEM)
    bf16, f32 = jnp.bfloat16, jnp.float32
    dma = pltpu.SemaphoreType.DMA
    half = quarters // 2
    return pl.pallas_call(
        functools.partial(reduce_kernel, owners, quarters),
        out_shape=(
            jax.ShapeDtypeStruct(weight_terms.shape, bf16),
            jax.ShapeDtypeStruct((owners, cap, sub, width), bf16),
        ),
        in_specs=[vmem, vmem],
        out_specs=(vmem, vmem),
        scratch_shapes=[
            pltpu.VMEM((PIECES, outer, piece, lanes), bf16),
            pltpu.VMEM((PIECES, outer, piece, lanes), bf16),
            pltpu.VMEM((PIECES, outer, piece, lanes), bf16),
            pltpu.VMEM((PIECES, piece, lanes), f32),
            pltpu.VMEM((levels, owners, half, cap, sub, width), bf16),
            pltpu.VMEM((levels, owners, half, cap, sub, width), bf16),
            pltpu.VMEM((owners, cap, sub, width), bf16),
            dma((2, PIECES, outer)),
            dma((2, PIECES, outer)),
            dma((2, PIECES, outer)),
            dma((2, PIECES, outer)),
            dma((2, levels, owners, half)),
            dma((2, owners)),
        ],
        compiler_params=pltpu.CompilerParams(
            collective_id=0, has_side_effects=True, vmem_limit_bytes=60 << 20
        ),
        cost_estimate=pl.CostEstimate(flops=1 << 24, bytes_accessed=16 << 20, transcendentals=0),
        name="reduce_all",
    )(weight_terms, slot_grads)


def fetch_kernel(
    owners, quarters, req_ref, cache_ref, keys_ref, asked_ref, packed, req_sem, get_sem, pass_sem
):
    f32, bf16 = jnp.float32, jnp.bfloat16
    s = lax.axis_index("seq")
    h = lax.axis_index("head")
    cap = packed.shape[1]
    sub = packed.shape[2]
    block_count = cache_ref.shape[1] // BLOCK
    bits = []
    while (1 << len(bits)) < quarters:
        bits.insert(0, 1 << len(bits))

    def flip(q, bit):
        return q + bit * (1 - 2 * lax.rem(q // bit, 2))

    def held(j):
        q = h
        for level, bit in enumerate(bits):
            if (j >> level) % 2:
                q = flip(q, bit)
        return q

    def owner(k):
        return lax.rem(s + k + 1, owners)

    def asker(k):
        return lax.rem(s + owners - k - 1, owners)

    def rows(q):
        return pl.ds(pl.multiple_of(q * sub, sub), sub)

    barrier = pltpu.get_barrier_semaphore()
    for k in range(owners - 1):
        pl.semaphore_signal(
            barrier, inc=1, device_id=(owner(k), h), device_id_type=pl.DeviceIdType.MESH
        )
    for bit in bits:
        pl.semaphore_signal(
            barrier, inc=1, device_id=(s, flip(h, bit)), device_id_type=pl.DeviceIdType.MESH
        )
    pl.semaphore_wait(barrier, owners - 1 + len(bits))

    def send(src, dst, sems, index, target):
        copy = pltpu.make_async_remote_copy(
            src_ref=src,
            dst_ref=dst,
            send_sem=sems.at[(0,) + index],
            recv_sem=sems.at[(1,) + index],
            device_id=target,
            device_id_type=pl.DeviceIdType.MESH,
        )
        copy.start()
        return copy

    req_copy, get_copy, pass_copy = {}, {}, {}
    for k in range(owners - 1):
        req_copy[k] = send(
            req_ref.at[owner(k)], asked_ref.at[s], req_sem, (k,), (owner(k), h)
        )

    def pick(ask, c):
        chosen = jnp.zeros((sub, BLOCK), f32)
        for b in range(block_count):
            part = cache_ref[rows(h), b * BLOCK : (b + 1) * BLOCK].astype(f32)
            chosen = jnp.where(ask[c : c + 1, :] == b, part, chosen)
        return chosen.astype(bf16)

    def hand_on(k, j):
        spot = keys_ref.at[pl.ds(owner(k) * cap, cap), rows(held(j))]
        for level in range(j.bit_length(), len(bits)):
            index = j + (1 << level)
            pass_copy[k, index] = send(
                spot, spot, pass_sem, (k, index), (s, flip(h, bits[level]))
            )

    last = owners - 1
    own = req_ref[s]
    asked_ref[s] = own
    for c in range(cap):
        keys_ref[s * cap + c, rows(h)] = pick(own, c)
    hand_on(last, 0)
    for k in range(owners - 1):
        req_copy[k].wait_recv()
        ask = asked_ref[asker(k)]
        for c in range(cap):
            packed[k, c] = pick(ask, c)
        get_copy[k] = send(
            packed.at[k],
            keys_ref.at[pl.ds(s * cap, cap), rows(h)],
            get_sem,
            (k,),
            (asker(k), h),
        )
    for k in range(-1, owners):
        if 0 <= k < last:
            get_copy[k].wait_recv()
            hand_on(k, 0)
        before = last if k == 0 else k - 1
        if k >= 0:
            for j in range(1, quarters):
                pass_copy[before, j].wait_recv()
                hand_on(before, j)
    for group in (req_copy, get_copy, pass_copy):
        for copy in group.values():
            copy.wait_send()


def fetch(owners, quarters, request, cache_t):
    width = cache_t.shape[0]
    cap = request.shape[1]
    vmem = pl.BlockSpec(memory_space=pltpu.VMEM)
    dma = pltpu.SemaphoreType.DMA
    padded = -(-cap // 8) * 8
    request = jnp.pad(request, ((0, 0), (0, padded - cap)), constant_values=-1)
    request = jnp.broadcast_to(request[:, :, None], (owners, padded, BLOCK))
    keys_t, asked = pl.pallas_call(
        functools.partial(fetch_kernel, owners, quarters),
        out_shape=(
            jax.ShapeDtypeStruct((owners * cap, width, BLOCK), cache_t.dtype),
            jax.ShapeDtypeStruct((owners, padded, BLOCK), jnp.int32),
        ),
        in_specs=[vmem, vmem],
        out_specs=(vmem, vmem),
        scratch_shapes=[
            pltpu.VMEM((owners, cap, width // quarters, BLOCK), cache_t.dtype),
            dma((2, owners)),
            dma((2, owners)),
            dma((2, owners, quarters)),
        ],
        compiler_params=pltpu.CompilerParams(
            collective_id=1, has_side_effects=True, vmem_limit_bytes=48 << 20
        ),
        cost_estimate=pl.CostEstimate(flops=1 << 22, bytes_accessed=4 << 20, transcendentals=0),
        name="fetch",
    )(request, cache_t)
    return keys_t, asked[:, :cap, 0].reshape(owners * cap)


def local(query, cache, grad_out, value_weight, picked):
    q_dev, heads_here, row_width = query.shape
    ctx_dev = cache.shape[0]
    owners = lax.axis_size("seq")
    seq_index = lax.axis_index("seq")
    quarters = lax.axis_size("head")
    block_count = ctx_dev // BLOCK
    qblocks_here = q_dev // QB
    entries = qblocks_here * TOPB
    capacity = max(q_dev // BLOCK, entries // owners)
    slot_total = owners * capacity
    sub_rows = BLOCK // quarters
    flat_pick = picked.reshape(entries)
    owner_of = flat_pick // block_count
    global_ids = jnp.arange(owners * block_count, dtype=jnp.int32)
    matches = flat_pick[:, None] == global_ids[None, :]
    wanted = jnp.any(matches, axis=0).astype(jnp.int32).reshape(owners, block_count)
    order_in = jnp.cumsum(wanted, axis=1) - 1
    slot_ids = jnp.arange(capacity, dtype=jnp.int32)
    local_ids = jnp.arange(block_count, dtype=jnp.int32)
    holding = (wanted[:, None, :] == 1) & (order_in[:, None, :] == slot_ids[None, :, None])
    present = jnp.any(holding, axis=2)
    request = jnp.where(
        present, jnp.sum(jnp.where(holding, local_ids[None, None, :], 0), axis=2), -1
    )
    entry_rank = jnp.sum(
        jnp.where(matches, order_in.reshape(owners * block_count)[None, :], 0), axis=1
    )
    entry_slot = owner_of * capacity + entry_rank
    keys_t, asked_rows = fetch(owners, quarters, request, cache.T)
    owner_map = (local_ids[:, None] == asked_rows[None, :]).astype(jnp.float32)
    first_pos = ctx_dev * owners - q_dev * owners + seq_index * q_dev
    rel = flat_pick * BLOCK - first_pos - (jnp.arange(entries, dtype=jnp.int32) // TOPB) * QB
    d_query_t, slot_grads, weight_terms = attention(
        entry_slot,
        rel,
        jnp.transpose(query, (1, 2, 0)),
        jnp.transpose(grad_out, (1, 0, 2)),
        value_weight,
        keys_t,
    )
    d_value_weight, returned = reduce_all(
        owners,
        quarters,
        weight_terms.reshape(owners, -1, weight_terms.shape[2]),
        slot_grads,
    )
    d_value_weight = d_value_weight.reshape(value_weight.shape)
    d_cache = jnp.dot(
        owner_map,
        returned.astype(jnp.float32).reshape(slot_total, sub_rows * row_width),
        precision=lax.Precision.HIGHEST,
    ).reshape(block_count, sub_rows, row_width)
    return (jnp.transpose(d_query_t, (2, 0, 1)), d_cache, d_value_weight)


def solution(mesh):
    in_specs = (
        P("seq", "head", None),
        P("seq", None),
        P("seq", "head", None),
        P("head", None, None),
        P("seq", None),
    )
    out_specs = (P("seq", "head", None), P("seq", "head", None), P("head", None, None))
    return jax.shard_map(local, mesh=mesh, in_specs=in_specs, out_specs=out_specs, check_vma=False)
```

```python
import functools

import jax
import jax.numpy as jnp
from jax import lax
from jax.experimental import pallas as pl
from jax.experimental.pallas import tpu as pltpu
from jax.sharding import PartitionSpec as P

KVL = 512
BLOCK = 128
QB = 32
TOPB = 4


SCORE_SCALE = 0.07216878364870323
MASKED = -1e30

NT = (((1,), (1,)), ((), ()))


def attention_kernel(
    slot_ref,
    rel_ref,
    q_ref,
    g_ref,
    w_ref,
    kt_ref,
    dq_ref,
    dk_ref,
    wt_ref,
    q_rows,
    dl_rows,
    lo_rows,
    dq_rows,
    kt_all,
    kn_all,
    dk_sum,
):
    heads, width, queries = q_ref.shape
    qblocks = queries // QB
    group = BLOCK // QB
    f32, bf16 = jnp.float32, jnp.bfloat16

    def spread(i, carry):
        lanes = pl.ds(pl.multiple_of(i * BLOCK, BLOCK), BLOCK)
        qs = [q_ref[i * group + j] for j in range(group)]
        ds = [
            lax.dot_general(
                w_ref[i * group + j], g_ref[i * group + j], NT, preferred_element_type=f32
            ).astype(bf16)
            for j in range(group)
        ]
        for g in range(qblocks):
            cut = slice(g * QB, (g + 1) * QB)
            q_rows[g, :, lanes] = jnp.concatenate([x[:, cut] for x in qs], axis=1)
            dl_rows[g, :, lanes] = jnp.concatenate([x[:, cut] for x in ds], axis=1)
        return carry

    lax.fori_loop(0, heads // group, spread, 0)
    dk_sum[...] = jnp.zeros_like(dk_sum)

    def block(g, carry):
        for t in range(TOPB):
            key_t = kt_ref[slot_ref[g * TOPB + t]]
            kt_all[:, t * BLOCK : (t + 1) * BLOCK] = key_t
            kn_all[t * BLOCK : (t + 1) * BLOCK, :] = key_t.T
        q_t = q_rows[g]
        dl_t = dl_rows[g]
        rows = q_t.shape[1]
        scores = jnp.dot(kn_all[...], q_t, preferred_element_type=f32) * SCORE_SCALE
        key_at = lax.broadcasted_iota(jnp.int32, (BLOCK, rows), 0)
        query_at = lax.rem(lax.broadcasted_iota(jnp.int32, (BLOCK, rows), 1), QB)
        ahead = key_at - query_at
        parts = []
        for t in range(TOPB):
            seen = ahead <= -rel_ref[g * TOPB + t]
            parts.append(jnp.where(seen, scores[t * BLOCK : (t + 1) * BLOCK], MASKED))
        scores = jnp.concatenate(parts, axis=0)
        top = jnp.max(scores, axis=0, keepdims=True)
        exps = jnp.exp(scores - top)
        weights = exps / jnp.sum(exps, axis=0, keepdims=True)
        low = weights.astype(bf16)
        latent = jnp.dot(kt_all[:KVL, :], low, preferred_element_type=f32).astype(bf16)
        lo_rows[g] = latent
        delta = jnp.sum(dl_t.astype(f32) * latent.astype(f32), axis=0, keepdims=True)
        d_probs = jnp.dot(kn_all[:, :KVL], dl_t, preferred_element_type=f32)
        d_scores = (SCORE_SCALE * weights * (d_probs - delta)).astype(bf16)
        dq_rows[g] = jnp.dot(kt_all[...], d_scores, preferred_element_type=f32).astype(bf16)
        d_keys = lax.dot_general(d_scores, q_t, NT, preferred_element_type=f32)
        d_values = lax.dot_general(low, dl_t, NT, preferred_element_type=f32)
        for t in range(TOPB):
            slot = slot_ref[g * TOPB + t]
            cut = slice(t * BLOCK, (t + 1) * BLOCK)
            dk_sum[slot, :, :KVL] += d_keys[cut, :KVL] + d_values[cut]
            dk_sum[slot, :, KVL:] += d_keys[cut, KVL:]
        return carry

    lax.fori_loop(0, qblocks, block, 0)
    dk_ref[...] = dk_sum[...].astype(dk_ref.dtype)

    def gather(i, carry):
        lanes = pl.ds(pl.multiple_of(i * BLOCK, BLOCK), BLOCK)
        qs = [dq_rows[g, :, lanes] for g in range(qblocks)]
        ls = [lo_rows[g, :, lanes] for g in range(qblocks)]
        for j in range(group):
            cut = slice(j * QB, (j + 1) * QB)
            dq_ref[i * group + j] = jnp.concatenate([x[:, cut] for x in qs], axis=1)
            latent = jnp.concatenate([x[:, cut] for x in ls], axis=1)
            wt_ref[i * group + j] = jnp.dot(
                latent, g_ref[i * group + j], preferred_element_type=f32
            ).astype(wt_ref.dtype)
        return carry

    lax.fori_loop(0, heads // group, gather, 0)


def attention(slots, rel, q_t, g_h, weight, keys_t):
    heads, width, queries = q_t.shape
    slot_total = keys_t.shape[0]
    qblocks = queries // QB
    rows = heads * QB
    macs = heads * queries * (TOPB * BLOCK * 3 * (width + KVL) + 2 * KVL * BLOCK)
    vmem = pl.BlockSpec(memory_space=pltpu.VMEM)
    smem = pl.BlockSpec(memory_space=pltpu.SMEM)
    bf16 = jnp.bfloat16
    return pl.pallas_call(
        attention_kernel,
        out_shape=(
            jax.ShapeDtypeStruct(q_t.shape, bf16),
            jax.ShapeDtypeStruct((slot_total, BLOCK, width), bf16),
            jax.ShapeDtypeStruct(weight.shape, bf16),
        ),
        in_specs=[smem, smem, vmem, vmem, vmem, vmem],
        out_specs=(vmem, vmem, vmem),
        scratch_shapes=[
            pltpu.VMEM((qblocks, width, rows), bf16),
            pltpu.VMEM((qblocks, KVL, rows), bf16),
            pltpu.VMEM((qblocks, KVL, rows), bf16),
            pltpu.VMEM((qblocks, width, rows), bf16),
            pltpu.VMEM((width, TOPB * BLOCK), bf16),
            pltpu.VMEM((TOPB * BLOCK, width), bf16),
            pltpu.VMEM((slot_total, BLOCK, width), jnp.float32),
        ],
        compiler_params=pltpu.CompilerParams(
            vmem_limit_bytes=(20 << 20) + slot_total * (640 << 10)
        ),
        cost_estimate=pl.CostEstimate(
            flops=2 * macs, bytes_accessed=16 << 20, transcendentals=rows * qblocks * 512
        ),
        name="attention",
    )(slots, rel, q_t, g_h, weight, keys_t)


PIECES = 4


def reduce_kernel(
    owners,
    quarters,
    w_ref,
    dk_ref,
    asked_ref,
    out_ref,
    cache_ref,
    ret_ref,
    y_buf,
    z_send,
    z_buf,
    mine,
    kept,
    half_buf,
    final,
    y_sem,
    z_sem,
    gz_sem,
    gy_sem,
    half_sem,
    ret_sem,
):
    f32, bf16 = jnp.float32, jnp.bfloat16
    s = lax.axis_index("seq")
    h = lax.axis_index("head")
    outer = owners // 2
    a, b = s // 2, lax.rem(s, 2)
    pair = a * 2 + 1 - b
    cap = ret_ref.shape[1]
    sub = ret_ref.shape[2]
    rows = w_ref.shape[1] // PIECES
    bits = []
    while (1 << len(bits)) < quarters:
        bits.append(1 << len(bits))

    def flipped(bit):
        return h + bit * (1 - 2 * lax.rem(h // bit, 2))

    barrier = pltpu.get_barrier_semaphore()
    for k in range(owners - 1):
        pl.semaphore_signal(
            barrier,
            inc=1,
            device_id=(lax.rem(s + k + 1, owners), h),
            device_id_type=pl.DeviceIdType.MESH,
        )
    for bit in bits:
        pl.semaphore_signal(
            barrier, inc=1, device_id=(s, flipped(bit)), device_id_type=pl.DeviceIdType.MESH
        )
    pl.semaphore_wait(barrier, owners - 1 + len(bits))

    def send(src, dst, sems, index, target):
        copy = pltpu.make_async_remote_copy(
            src_ref=src,
            dst_ref=dst,
            send_sem=sems.at[(0,) + index],
            recv_sem=sems.at[(1,) + index],
            device_id=target,
            device_id_type=pl.DeviceIdType.MESH,
        )
        copy.start()
        return copy

    def ahead(k):
        return lax.rem(a + k + 1, outer)

    def behind(k):
        return lax.rem(a + outer - k - 1, outer)

    def owner(k):
        return lax.rem(s + k + 1, owners)

    cuts = [pl.ds(p * rows, rows) for p in range(PIECES)]
    y_copy, z_copy, gz_copy, gy_copy = {}, {}, {}, {}
    half_copy, ret_copy = {}, {}

    first = bits[0]
    low = lax.rem(h, 2)
    for k in range(outer):
        y_copy[0, k] = send(
            w_ref.at[ahead(k) * 2 + 1 - b, cuts[0]], y_buf.at[0, k], y_sem, (0, k), (pair, h)
        )
    for k in range(owners):
        slots = pl.ds(owner(k) * cap, cap)
        for i in range(quarters // 2):
            q = 2 * i + 1 - low
            half_copy[0, k, i] = send(
                dk_ref.at[slots, pl.ds(pl.multiple_of(q * sub, sub), sub)],
                half_buf.at[0, k, i],
                half_sem,
                (0, k, i),
                (s, flipped(first)),
            )
    for p in range(1, PIECES):
        for k in range(outer):
            y_copy[p, k] = send(
                w_ref.at[ahead(k) * 2 + 1 - b, cuts[p]], y_buf.at[p, k], y_sem, (p, k), (pair, h)
            )

    def halve(level, k):
        bit = bits[level]
        count = quarters // (2 * bit)
        for i in range(count):
            half_copy[level, k, i].wait_recv()
            if level == 0:
                q = 2 * i + low
                here = dk_ref[
                    pl.ds(owner(k) * cap, cap), pl.ds(pl.multiple_of(q * sub, sub), sub)
                ].astype(f32)
            else:
                here = kept[level - 1, k, 2 * i + lax.rem(h // bit, 2)].astype(f32)
            here = here + half_buf[level, k, i].astype(f32)
            if level + 1 < len(bits):
                kept[level, k, i] = here.astype(bf16)
        if level + 1 < len(bits):
            after = bits[level + 1]
            for i in range(count // 2):
                other = 2 * i + 1 - lax.rem(h // after, 2)
                half_copy[level + 1, k, i] = send(
                    kept.at[level, k, other],
                    half_buf.at[level + 1, k, i],
                    half_sem,
                    (level + 1, k, i),
                    (s, flipped(after)),
                )
        elif k < owners - 1:
            final[k] = here.astype(bf16)
            ret_copy[k] = send(final.at[k], ret_ref.at[s], ret_sem, (k,), (owner(k), h))
        else:
            ret_ref[s] = here.astype(bf16)

    def paired(p):
        for k in range(outer):
            y_copy[p, k].wait_recv()
            part = w_ref[ahead(k) * 2 + b, cuts[p]].astype(f32) + y_buf[p, k].astype(f32)
            if k < outer - 1:
                z_send[p, k] = part.astype(bf16)
                z_copy[p, k] = send(
                    z_send.at[p, k], z_buf.at[p, k], z_sem, (p, k), (ahead(k) * 2 + b, h)
                )
            else:
                mine[p] = part

    def totalled(p):
        total = mine[p]
        for k in range(outer - 1):
            z_copy[p, k].wait_recv()
            total = total + z_buf[p, k].astype(f32)
        out_ref[s, cuts[p]] = total.astype(bf16)
        spot = out_ref.at[s, cuts[p]]
        for k in range(outer - 1):
            gz_copy[p, k] = send(spot, spot, gz_sem, (p, k), (ahead(k) * 2 + b, h))
        gy_copy[p, outer - 1] = send(spot, spot, gy_sem, (p, outer - 1), (pair, h))

    def forwarded(p):
        for k in range(outer - 1):
            gz_copy[p, k].wait_recv()
            spot = out_ref.at[behind(k) * 2 + b, cuts[p]]
            gy_copy[p, k] = send(spot, spot, gy_sem, (p, k), (pair, h))

    for level in range(len(bits) - 1):
        for k in range(owners):
            halve(level, k)
    share = -(-owners // PIECES)
    for p in range(PIECES):
        paired(p)
        for k in range(p * share, min(owners, (p + 1) * share)):
            halve(len(bits) - 1, k)
        if p >= 1:
            totalled(p - 1)
        if p >= 2:
            forwarded(p - 2)
    totalled(PIECES - 1)
    for p in range(max(0, PIECES - 2), PIECES):
        forwarded(p)
    for copy in ret_copy.values():
        copy.wait_recv()
    for block in range(cache_ref.shape[0]):
        total = jnp.zeros(cache_ref.shape[1:], f32)
        for o in range(owners):
            for c in range(cap):
                here = asked_ref[o, c : c + 1, 0:1] == block
                total = total + jnp.where(here, ret_ref[o, c].astype(f32), 0.0)
        cache_ref[block] = total
    for copy in gy_copy.values():
        copy.wait_recv()
    for group in (y_copy, z_copy, gz_copy, gy_copy, half_copy, ret_copy):
        for copy in group.values():
            copy.wait_send()


def reduce_all(owners, quarters, block_count, weight_terms, slot_grads, asked):
    _, rows, lanes = weight_terms.shape
    slot_total, block, width = slot_grads.shape
    cap = slot_total // owners
    sub = block // quarters
    outer = owners // 2
    levels = max(1, quarters.bit_length() - 1)
    piece = rows // PIECES
    vmem = pl.BlockSpec(memory_space=pltpu.VMEM)
    bf16, f32 = jnp.bfloat16, jnp.float32
    dma = pltpu.SemaphoreType.DMA
    half = quarters // 2
    return pl.pallas_call(
        functools.partial(reduce_kernel, owners, quarters),
        out_shape=(
            jax.ShapeDtypeStruct(weight_terms.shape, bf16),
            jax.ShapeDtypeStruct((block_count, sub, width), f32),
        ),
        in_specs=[vmem, vmem, vmem],
        out_specs=(vmem, vmem),
        scratch_shapes=[
            pltpu.VMEM((owners, cap, sub, width), bf16),
            pltpu.VMEM((PIECES, outer, piece, lanes), bf16),
            pltpu.VMEM((PIECES, outer, piece, lanes), bf16),
            pltpu.VMEM((PIECES, outer, piece, lanes), bf16),
            pltpu.VMEM((PIECES, piece, lanes), f32),
            pltpu.VMEM((levels, owners, half, cap, sub, width), bf16),
            pltpu.VMEM((levels, owners, half, cap, sub, width), bf16),
            pltpu.VMEM((owners, cap, sub, width), bf16),
            dma((2, PIECES, outer)),
            dma((2, PIECES, outer)),
            dma((2, PIECES, outer)),
            dma((2, PIECES, outer)),
            dma((2, levels, owners, half)),
            dma((2, owners)),
        ],
        compiler_params=pltpu.CompilerParams(
            collective_id=0,
            has_side_effects=True,
            vmem_limit_bytes=(12 << 20) + slot_total * (750 << 10),
        ),
        cost_estimate=pl.CostEstimate(flops=1 << 24, bytes_accessed=16 << 20, transcendentals=0),
        name="reduce_all",
    )(weight_terms, slot_grads, asked)


def fetch_kernel(
    owners, quarters, req_ref, cache_ref, keys_ref, asked_ref, packed, req_sem, get_sem, pass_sem
):
    f32, bf16 = jnp.float32, jnp.bfloat16
    s = lax.axis_index("seq")
    h = lax.axis_index("head")
    cap = packed.shape[1]
    sub = packed.shape[2]
    block_count = cache_ref.shape[1] // BLOCK
    bits = []
    while (1 << len(bits)) < quarters:
        bits.insert(0, 1 << len(bits))

    def flip(q, bit):
        return q + bit * (1 - 2 * lax.rem(q // bit, 2))

    def held(j):
        q = h
        for level, bit in enumerate(bits):
            if (j >> level) % 2:
                q = flip(q, bit)
        return q

    def owner(k):
        return lax.rem(s + k + 1, owners)

    def asker(k):
        return lax.rem(s + owners - k - 1, owners)

    def rows(q):
        return pl.ds(pl.multiple_of(q * sub, sub), sub)

    barrier = pltpu.get_barrier_semaphore()
    for k in range(owners - 1):
        pl.semaphore_signal(
            barrier, inc=1, device_id=(owner(k), h), device_id_type=pl.DeviceIdType.MESH
        )
    for bit in bits:
        pl.semaphore_signal(
            barrier, inc=1, device_id=(s, flip(h, bit)), device_id_type=pl.DeviceIdType.MESH
        )
    pl.semaphore_wait(barrier, owners - 1 + len(bits))

    def send(src, dst, sems, index, target):
        copy = pltpu.make_async_remote_copy(
            src_ref=src,
            dst_ref=dst,
            send_sem=sems.at[(0,) + index],
            recv_sem=sems.at[(1,) + index],
            device_id=target,
            device_id_type=pl.DeviceIdType.MESH,
        )
        copy.start()
        return copy

    req_copy, get_copy, pass_copy = {}, {}, {}
    for k in range(owners - 1):
        req_copy[k] = send(
            req_ref.at[owner(k)], asked_ref.at[s], req_sem, (k,), (owner(k), h)
        )

    def pick(ask, c):
        chosen = jnp.zeros((sub, BLOCK), f32)
        for b in range(block_count):
            part = cache_ref[rows(h), b * BLOCK : (b + 1) * BLOCK].astype(f32)
            chosen = jnp.where(ask[c : c + 1, :] == b, part, chosen)
        return chosen.astype(bf16)

    def hand_on(k, j):
        spot = keys_ref.at[pl.ds(owner(k) * cap, cap), rows(held(j))]
        for level in range(j.bit_length(), len(bits)):
            index = j + (1 << level)
            pass_copy[k, index] = send(
                spot, spot, pass_sem, (k, index), (s, flip(h, bits[level]))
            )

    last = owners - 1
    own = req_ref[s]
    asked_ref[s] = own
    for c in range(cap):
        keys_ref[s * cap + c, rows(h)] = pick(own, c)
    hand_on(last, 0)
    for k in range(owners - 1):
        req_copy[k].wait_recv()
        ask = asked_ref[asker(k)]
        for c in range(cap):
            packed[k, c] = pick(ask, c)
        get_copy[k] = send(
            packed.at[k],
            keys_ref.at[pl.ds(s * cap, cap), rows(h)],
            get_sem,
            (k,),
            (asker(k), h),
        )
    for k in range(-1, owners):
        if 0 <= k < last:
            get_copy[k].wait_recv()
            hand_on(k, 0)
        before = last if k == 0 else k - 1
        if k >= 0:
            for j in range(1, quarters):
                pass_copy[before, j].wait_recv()
                hand_on(before, j)
    for group in (req_copy, get_copy, pass_copy):
        for copy in group.values():
            copy.wait_send()


def fetch(owners, quarters, request, cache_t):
    width = cache_t.shape[0]
    cap = request.shape[1]
    vmem = pl.BlockSpec(memory_space=pltpu.VMEM)
    dma = pltpu.SemaphoreType.DMA
    padded = -(-cap // 8) * 8
    request = jnp.pad(request, ((0, 0), (0, padded - cap)), constant_values=-1)
    request = jnp.broadcast_to(request[:, :, None], (owners, padded, BLOCK))
    keys_t, asked = pl.pallas_call(
        functools.partial(fetch_kernel, owners, quarters),
        out_shape=(
            jax.ShapeDtypeStruct((owners * cap, width, BLOCK), cache_t.dtype),
            jax.ShapeDtypeStruct((owners, padded, BLOCK), jnp.int32),
        ),
        in_specs=[vmem, vmem],
        out_specs=(vmem, vmem),
        scratch_shapes=[
            pltpu.VMEM((owners, cap, width // quarters, BLOCK), cache_t.dtype),
            dma((2, owners)),
            dma((2, owners)),
            dma((2, owners, quarters)),
        ],
        compiler_params=pltpu.CompilerParams(
            collective_id=1,
            has_side_effects=True,
            vmem_limit_bytes=(8 << 20) + owners * cap * (256 << 10),
        ),
        cost_estimate=pl.CostEstimate(flops=1 << 22, bytes_accessed=4 << 20, transcendentals=0),
        name="fetch",
    )(request, cache_t)
    return keys_t, asked


def local(query, cache, grad_out, value_weight, picked):
    q_dev, heads_here, row_width = query.shape
    ctx_dev = cache.shape[0]
    owners = lax.axis_size("seq")
    seq_index = lax.axis_index("seq")
    quarters = lax.axis_size("head")
    block_count = ctx_dev // BLOCK
    qblocks_here = q_dev // QB
    entries = qblocks_here * TOPB
    capacity = max(q_dev // BLOCK, entries // owners)
    slot_total = owners * capacity
    sub_rows = BLOCK // quarters
    flat_pick = picked.reshape(entries)
    owner_of = flat_pick // block_count
    global_ids = jnp.arange(owners * block_count, dtype=jnp.int32)
    matches = flat_pick[:, None] == global_ids[None, :]
    wanted = jnp.any(matches, axis=0).astype(jnp.int32).reshape(owners, block_count)
    order_in = jnp.cumsum(wanted, axis=1) - 1
    slot_ids = jnp.arange(capacity, dtype=jnp.int32)
    local_ids = jnp.arange(block_count, dtype=jnp.int32)
    holding = (wanted[:, None, :] == 1) & (order_in[:, None, :] == slot_ids[None, :, None])
    present = jnp.any(holding, axis=2)
    request = jnp.where(
        present, jnp.sum(jnp.where(holding, local_ids[None, None, :], 0), axis=2), -1
    )
    entry_rank = jnp.sum(
        jnp.where(matches, order_in.reshape(owners * block_count)[None, :], 0), axis=1
    )
    entry_slot = owner_of * capacity + entry_rank
    keys_t, asked = fetch(owners, quarters, request, cache.T)
    first_pos = ctx_dev * owners - q_dev * owners + seq_index * q_dev
    rel = flat_pick * BLOCK - first_pos - (jnp.arange(entries, dtype=jnp.int32) // TOPB) * QB
    d_query_t, slot_grads, weight_terms = attention(
        entry_slot,
        rel,
        jnp.transpose(query, (1, 2, 0)),
        jnp.transpose(grad_out, (1, 0, 2)),
        value_weight,
        keys_t,
    )
    d_value_weight, d_cache = reduce_all(
        owners,
        quarters,
        block_count,
        weight_terms.reshape(owners, -1, weight_terms.shape[2]),
        slot_grads,
        asked,
    )
    d_value_weight = d_value_weight.reshape(value_weight.shape)
    return (jnp.transpose(d_query_t, (2, 0, 1)), d_cache, d_value_weight)


def solution(mesh):
    in_specs = (
        P("seq", "head", None),
        P("seq", None),
        P("seq", "head", None),
        P("head", None, None),
        P("seq", None),
    )
    out_specs = (P("seq", "head", None), P("seq", "head", None), P("head", None, None))
    return jax.shard_map(local, mesh=mesh, in_specs=in_specs, out_specs=out_specs, check_vma=False)
```
